32 devices in a mesh: groups: 2 (over x), tensor: 16 (over z, y, core).
Axes of the slice: x: 2, y: 2, z: 4, core: 2. Of those that a mesh axis runs over, the one named last changes fastest.
Arguments:
- tokens: bfloat16 [24576, 8192], P(('groups', 'tensor')), parts along dimension 0, may hold values from -6 to 6
- norm_gain: float32 [8192], replicated, may hold values from 0.25 to 1.75
- w_kv: bfloat16 [8192, 1024], P('tensor'), may hold values from -0.0625 to 0.0625
- w_out: bfloat16 [4096, 8192], P(None, 'tensor'), may hold values from -0.09375 to 0.09375
- lengths: int32 [48], P('groups'), parts along dimension 0, may hold values from 1 to 512, 7680 in all
- request_owner: int32 [48], P('groups'), parts along dimension 0, may hold values from 0 to 15, as said below
- block_table: int32 [192], P('groups'), parts along dimension 0, may hold values from 0 to 95, as said below
- dec_query: bfloat16 [64, 4, 4096], P(('groups', 'tensor')), parts along dimension 0, may hold values from -400 to 400
- dec_new: bfloat16 [64, 4, 1024], P(('groups', 'tensor')), parts along dimension 0, may hold values from -5 to 5
Outputs:
- decoded: bfloat16 [64, 4, 8192], P('groups', None, 'tensor'), parts along dimension 0
The draws below stay inside these ranges and needn't reach their ends.
There are 2 independent parts, one for each index of `groups`. The reference program is written for one: setup_inputs(seed, part) draws one part's arguments, and reference() takes and returns one part's arrays. A program takes and returns all parts, laid end to end along the dimension named above; an argument that names none is the same for every part. Nothing has to cross between parts.
Inputs may be any that keep to these rules, and one draw needn't show every extreme that they name: `request_owner`: no index of tensor owns more than 2 requests, and one owns exactly 2. block_table[r * 4 + j] is the pool block that holds positions j * 128 to (j + 1) * 128 - 1 of request r; every pool block appears once; the 6 pool blocks d * 6 to (d + 1) * 6 - 1 of one index d of tensor hold at most one block of the requests of any one owner.
All inputs are finite; a program needn't handle non-finite values.
Results may differ from the reference program's by a relative error of at most 0.0081.
Values may be sent and summed in bfloat16 or wider, within the bound.
No kernel may reach another device: no remote copies, remote signals or barrier semaphores. Data moves between devices by JAX's collectives and lax.ppermute only.
A program may use at most 128 MiB of HBM per device.

```python
import math
import jax
import jax.numpy as jnp
import numpy as np
from jax import lax

D = 8192
QH = 32
KVH = 4
HD = 128
BLK = 128
MAXBLK = 4
STEPS = 4
OWN_MAX = 2
BLK_DEV = 6
MAXLEN = 512
NBLK = 96
PTOK = 12288
REQS = 24
SLOTS = 32
TOTAL_LEN = 7680
N_TENSOR = 16


def fresh_normals(key):
    return jnp.clip(jax.random.normal(jax.random.fold_in(key, 41), (SLOTS, STEPS, 2 * KVH * HD), jnp.float32), -5.0, 5.0)


def owner_table(key):
    key = jax.random.fold_in(key, 3)
    keys_list = jax.random.split(key, 3)
    busiest = jax.random.randint(keys_list[0], (), 0, N_TENSOR)
    spare_slots = jax.random.permutation(keys_list[1], (N_TENSOR - 1) * OWN_MAX)[:REQS - OWN_MAX] // OWN_MAX
    others = (busiest + 1 + spare_slots) % N_TENSOR
    listed = jnp.concatenate([jnp.full((OWN_MAX,), busiest, jnp.int32), others.astype(jnp.int32)])
    shuffle = jax.random.permutation(keys_list[2], REQS)
    return listed[shuffle].astype(jnp.int32)


def draw_request_owner(key, part):
    return owner_table(key)


def draw_block_table(key, part):
    owners = owner_table(key)
    key = jax.random.fold_in(key, 13)
    keys_list = jax.random.split(key, 4)
    owner_rank = jax.random.permutation(keys_list[0], N_TENSOR).astype(jnp.int32)
    scores = owner_rank[owners] * REQS + jnp.arange(REQS, dtype=jnp.int32)
    order = jnp.argsort(scores, stable=True).astype(jnp.int32)
    place = jnp.argsort(order, stable=True).astype(jnp.int32)
    serial = place[:, None] * MAXBLK + jnp.arange(MAXBLK, dtype=jnp.int32)[None, :]
    device_perm = jax.random.permutation(keys_list[1], N_TENSOR).astype(jnp.int32)
    device = device_perm[serial % N_TENSOR]
    row_perm = jax.random.permutation(keys_list[2], BLK_DEV).astype(jnp.int32)
    shifts = jax.random.randint(keys_list[3], (N_TENSOR,), 0, BLK_DEV).astype(jnp.int32)
    within = (row_perm[serial // N_TENSOR] + shifts[device]) % BLK_DEV
    return (device * BLK_DEV + within).reshape(NBLK).astype(jnp.int32)


def draw_dec_new(key, part):
    shared = fresh_normals(key)
    return shared.astype(jnp.bfloat16)


def draw_dec_query(key, part):
    key = jax.random.fold_in(key, 7)
    queries = jnp.clip(jax.random.normal(key, (SLOTS, STEPS, QH * HD), jnp.float32), -5.0, 5.0)
    return queries.astype(jnp.bfloat16)


def shard_levels(own_key, shape, pieces, smallest, top_value):
    loudness = 1.0
    for position, shards_of in pieces:
        heights = jax.random.uniform(jax.random.fold_in(jax.random.fold_in(own_key, 6), position), (shards_of,), jnp.float32, smallest / len(pieces), top_value / len(pieces))
        loudness = loudness * jnp.repeat(jnp.exp(heights), shape[position] // shards_of).reshape((-1,) + (1,) * (len(shape) - 1 - position))
    return loudness


def profile(amount, total, bound, skew):
    portions = [(1 << 20) // math.isqrt(standing ** skew) + 1 for standing in range(2, amount + 1)]
    surplus, holding = total - bound - (amount - 1), [1] * (amount - 1)
    while surplus > 0:
        candidates = [i for i in range(amount - 1) if holding[i] < bound]
        pool, remaining = sum([portions[i] for i in candidates]), surplus
        for i in candidates:
            more = min(bound - holding[i], max(1, remaining * portions[i] // pool), surplus)
            holding[i] = holding[i] + more
            surplus = surplus - more
    return np.array([bound] + holding)


def uneven_parts(rng, number_of, total, bound, lean):
    if number_of == 2:
        one = jax.random.randint(rng, (), max(1, total - bound), min(bound, total - 1) + 1)
        return jnp.stack([one, total - one])
    sizes = jnp.asarray(profile(number_of, total, bound, lean), jnp.int32)
    twos = (number_of - 1) // 2
    giver, taker = sizes[1:1 + 2 * twos:2], sizes[2:2 + 2 * twos:2]
    margin = jnp.minimum(giver - 1, bound - taker)
    shifted = jax.random.randint(jax.random.fold_in(rng, 1), (twos,), 0, 1 << 20) % (margin + 1)
    sizes = sizes.at[1:1 + 2 * twos:2].set(giver - shifted).at[2:2 + 2 * twos:2].set(taker + shifted)
    return sizes[jax.random.permutation(jax.random.fold_in(rng, 2), number_of)]


def noise(rng, extent, spread, reach, shards=(), kind=jnp.bfloat16):
    array = jax.random.normal(rng, extent, jnp.float32) * spread
    if len(shards) > 0:
        array = shard_levels(rng, extent, shards, -0.22, 0.18) * array
    return jnp.clip(array, min=-reach, max=reach).astype(kind)


def setup_inputs(seed: int = 0, part: int = 0) -> dict:
    arg_keys = jax.random.split(jax.random.key(seed), 10)
    own_keys = jax.random.split(jax.random.fold_in(arg_keys[9], part), 10)
    return {
        "tokens": noise(own_keys[0], (PTOK, D), 1.0, 6.0, ((0, 16),)),
        "norm_gain": jnp.clip(1.0 + 0.15 * jax.random.normal(arg_keys[1], (D,), jnp.float32), 0.25, 1.75),
        "w_kv": noise(arg_keys[2], (D, 2 * KVH * HD), D ** -0.5, 0.0625, ((0, 16),)),
        "w_out": noise(arg_keys[3], (QH * HD, D), (QH * HD) ** -0.5, 0.09375, ((1, 16),)),
        "lengths": uneven_parts(own_keys[4], REQS, TOTAL_LEN, MAXLEN, 1).astype(jnp.int32),
        "request_owner": draw_request_owner(jax.random.fold_in(jax.random.fold_in(arg_keys[9], part), 71), part),
        "block_table": draw_block_table(jax.random.fold_in(jax.random.fold_in(arg_keys[9], part), 71), part),
        "dec_query": draw_dec_query(jax.random.fold_in(jax.random.fold_in(arg_keys[9], part), 71), part),
        "dec_new": draw_dec_new(jax.random.fold_in(jax.random.fold_in(arg_keys[9], part), 71), part),
    }


norm_eps = 1e-05
masked_score = -1e+30

def slot_tables(request_owner, lengths, block_table, slot_count):
    req_count = request_owner.shape[0]
    req_index = jnp.arange(req_count, dtype=jnp.int32)
    earlier = (request_owner[None, :] == request_owner[:, None]) & (req_index[None, :] < req_index[:, None])
    owner_rank = lax.optimization_barrier(jnp.sum(earlier.astype(jnp.int32), axis=1))
    slot_of = request_owner * OWN_MAX + owner_rank
    slot_hit = (slot_of[None, :] == jnp.arange(slot_count, dtype=jnp.int32)[:, None]).astype(jnp.int32)
    slot_live = lax.optimization_barrier(jnp.sum(slot_hit, axis=1))
    slot_len = lax.optimization_barrier(jnp.sum(slot_hit * lengths[None, :], axis=1))
    req_blocks = block_table.reshape(req_count, MAXBLK)
    source = lax.optimization_barrier(jnp.sum(slot_hit[:, :, None] * req_blocks[None, :, :], axis=1))
    return (slot_live, source, slot_len)

def attend(dec_query, dec_new, cached, slot_len, slot_live):
    slot_rows = dec_query.shape[0]
    group = QH // KVH
    queries = dec_query.astype(jnp.float32).reshape(slot_rows, STEPS, KVH, group, HD)
    cache_keys = cached[:, 0].astype(jnp.float32)
    cache_values = cached[:, 1].astype(jnp.float32)
    new_keys = dec_new[:, :, :KVH * HD].astype(jnp.float32).reshape(slot_rows, STEPS, KVH, HD)
    new_values = dec_new[:, :, KVH * HD:].astype(jnp.float32).reshape(slot_rows, STEPS, KVH, HD)
    score_scale = HD ** (-0.5)
    highest_prec = lax.Precision.HIGHEST
    past = jnp.einsum('nikgd,nktd->nikgt', queries, cache_keys, precision=highest_prec) * score_scale
    positions = jnp.arange(cache_keys.shape[2], dtype=jnp.int32)
    visible = positions[None, :] < slot_len[:, None]
    past = jnp.where(visible[:, None, None, None, :], past, masked_score)
    recent = jnp.einsum('nikgd,njkd->nikgj', queries, new_keys, precision=highest_prec) * score_scale
    step_index = jnp.arange(STEPS, dtype=jnp.int32)
    causal = step_index[None, :] <= step_index[:, None]
    recent = jnp.where(causal[None, :, None, None, :], recent, masked_score)
    highest = jnp.maximum(lax.optimization_barrier(jnp.max(past, axis=-1)), lax.optimization_barrier(jnp.max(recent, axis=-1)))
    past_exp = jnp.exp(past - highest[..., None])
    recent_exp = jnp.exp(recent - highest[..., None])
    total = lax.optimization_barrier(jnp.sum(past_exp, axis=-1)) + lax.optimization_barrier(jnp.sum(recent_exp, axis=-1))
    past_probs = (past_exp / total[..., None]).astype(jnp.bfloat16).astype(jnp.float32)
    recent_probs = (recent_exp / total[..., None]).astype(jnp.bfloat16).astype(jnp.float32)
    mixed = jnp.einsum('nikgt,nktd->nikgd', past_probs, cache_values, precision=highest_prec)
    mixed = mixed + jnp.einsum('nikgj,njkd->nikgd', recent_probs, new_values, precision=highest_prec)
    mixed = mixed * slot_live.astype(jnp.float32)[:, None, None, None, None]
    return mixed.reshape(slot_rows, STEPS, QH * HD).astype(jnp.bfloat16)

def reference(tokens, norm_gain, w_kv, w_out, lengths, request_owner, block_table, dec_query, dec_new):
    wide_tokens = tokens.astype(jnp.float32)
    inverse = lax.rsqrt(lax.optimization_barrier(jnp.mean(wide_tokens * wide_tokens, axis=1, keepdims=True)) + norm_eps)
    normed = (wide_tokens * inverse * norm_gain).astype(jnp.bfloat16)
    kv_rows = jnp.dot(normed, w_kv, preferred_element_type=jnp.float32).astype(jnp.bfloat16)
    slot_count = OWN_MAX * N_TENSOR
    slot_live, source, slot_len = slot_tables(request_owner, lengths, block_table, slot_count)
    blocks = kv_rows.reshape(NBLK, BLK, 2, KVH, HD)
    cached = blocks[source.reshape(-1)].reshape(slot_count, MAXBLK, BLK, 2, KVH, HD)
    cached = cached.transpose(0, 3, 4, 1, 2, 5).reshape(slot_count, 2, KVH, MAXBLK * BLK, HD)
    attended = attend(dec_query, dec_new, cached, slot_len, slot_live)
    flat_rows = attended.reshape(slot_count * STEPS, QH * HD)
    decoded = jnp.dot(flat_rows, w_out, preferred_element_type=jnp.float32).astype(jnp.bfloat16)
    return decoded.reshape(slot_count, STEPS, D)
```

```python
import functools

import jax
import jax.numpy as jnp
from jax import lax
from jax.experimental import pallas as pl
from jax.experimental.pallas import tpu as pltpu
from jax.sharding import PartitionSpec as P

QH = 32
KVH = 4
HD = 128
BLK = 128
MAXBLK = 4
STEPS = 4
OWN_MAX = 2
CORES = 2
LOCAL_KV = KVH // CORES
GROUP = QH // KVH
ROWS = GROUP * STEPS
LOCAL_ROWS = LOCAL_KV * ROWS
OWN_ROWS = 2 * LOCAL_KV * STEPS
QROWS = LOCAL_ROWS + OWN_ROWS
STAT_ROWS = 16

norm_eps = 1e-05
masked_score = -1e30
VMEM_LIMIT = 48 * 1024 * 1024


class Links:
    def __init__(self, groups, tensor):
        self.groups, self.tensor = groups, tensor
        self.nz = tensor // 4

    def move(self, value, kind, hops=1):
        pairs = []
        for g in range(self.groups):
            for t in range(self.tensor):
                to_g, to_t = g, t
                if kind == "c":
                    to_t = t ^ 1
                elif kind == "y":
                    to_t = t ^ 2
                elif kind == "yc":
                    to_t = t ^ 3
                elif kind == "z":
                    to_t = (t + 4 * hops) % self.tensor
                else:
                    to_g = g ^ 1
                pairs.append((g * self.tensor + t, to_g * self.tensor + to_t))
        return lax.ppermute(value, ("groups", "tensor"), pairs)


def tied(value, others):
    if not others:
        return value
    return lax.optimization_barrier((value,) + tuple(others))[0]


def split_columns(w_kv, core, half):
    rows, width = w_kv.shape
    part = width // (2 * CORES)
    gran = rows // 2

    def kernel(core_ref, half_ref, a, b, c, d, out_a, out_b, out_c, out_d):
        for src, dst in ((a, out_a), (b, out_b), (c, out_c), (d, out_d)):
            dst[...] = src[...]

    whole, halved = pl.BlockSpec((rows, part), lambda j, c, h: (0, j)), pl.BlockSpec(
        (gran, part), lambda j, c, h: (0, j)
    )
    return pl.pallas_call(
        kernel,
        grid_spec=pltpu.PrefetchScalarGridSpec(
            num_scalar_prefetch=2,
            grid=(2,),
            in_specs=[
                pl.BlockSpec((rows, part), lambda j, c, h: (0, CORES * j + c[0])),
                pl.BlockSpec((rows, part), lambda j, c, h: (0, CORES * j + 1 - c[0])),
                pl.BlockSpec((gran, part), lambda j, c, h: (h[0], CORES * j + c[0])),
                pl.BlockSpec((gran, part), lambda j, c, h: (h[0], CORES * j + 1 - c[0])),
            ],
            out_specs=[whole, whole, halved, halved],
        ),
        out_shape=[
            jax.ShapeDtypeStruct((n, 2 * part), w_kv.dtype) for n in (rows, rows, gran, gran)
        ],
        name="split",
    )(core.reshape(1), half.reshape(1), w_kv, w_kv, w_kv, w_kv)


def scale_kernel(chunk, tok_ref, out_ref):
    width = tok_ref.shape[1]
    acc = None
    for c in range(0, width, chunk):
        wide = tok_ref[:, c : c + chunk].astype(jnp.float32)
        acc = wide * wide if acc is None else acc + wide * wide
    inverse = lax.rsqrt(jnp.sum(acc, axis=1, keepdims=True) / width + norm_eps)
    out_ref[...] = jnp.broadcast_to(inverse, out_ref.shape)


def row_scale(tokens):
    rows, width = tokens.shape
    tile = 128
    return pl.pallas_call(
        functools.partial(scale_kernel, 512),
        grid=(rows // tile,),
        in_specs=[pl.BlockSpec((tile, width), lambda i: (i, 0))],
        out_specs=pl.BlockSpec((tile, 128), lambda i: (i, 0)),
        out_shape=jax.ShapeDtypeStruct((rows, 128), jnp.float32),
        compiler_params=pltpu.CompilerParams(vmem_limit_bytes=VMEM_LIMIT),
        cost_estimate=pl.CostEstimate(
            flops=2 * rows * width, bytes_accessed=2 * rows * width, transcendentals=rows
        ),
        name="row_scale",
    )(tokens)


def partial_sum(acc, lhs, scale_ref, gains, pieces, granules):
    scale = scale_ref[:, :1]
    at = 0
    for ref, count in zip(pieces, granules):
        size = ref.shape[0] // count
        for j in range(count):
            wide = lhs[at][...].astype(jnp.float32)
            normed = (wide * scale * gains[at][...]).astype(jnp.bfloat16)
            term = jnp.dot(
                normed, ref[j * size : (j + 1) * size, :], preferred_element_type=jnp.float32
            )
            acc = term if acc is None else acc + term
            at += 1
    return acc


def project_kernel(has_acc, granules, tiles, offs_ref, *refs):
    n = sum(granules)
    lead = 1 if has_acc else 0
    own, other = refs[lead : lead + n], refs[lead + n : lead + 2 * n]
    gains = refs[lead + 2 * n : lead + 3 * n]
    own_scale, other_scale = refs[lead + 3 * n : lead + 3 * n + 2]
    pieces, out_ref = refs[lead + 3 * n + 2 : -1], refs[-1]
    i = pl.program_id(0)

    def run(lhs, scale_ref):
        acc = refs[0][...] if has_acc else None
        out_ref[...] = partial_sum(acc, lhs, scale_ref, gains, pieces, granules)

    @pl.when(i < tiles)
    def _():
        run(own, own_scale)

    @pl.when(i >= tiles)
    def _():
        run(other, other_scale)


def token_specs(tile, tiles, gran, n):
    def own_row(i):
        return jnp.minimum(i, tiles - 1)

    def other_row(i):
        return jnp.maximum(i - tiles, 0)

    specs = []
    for row in (own_row, other_row):
        for j in range(n):
            specs.append(
                pl.BlockSpec((tile, gran), lambda i, s, *_, j=j, row=row: (row(i), s[j]))
            )
    for j in range(n):
        specs.append(pl.BlockSpec((1, gran), lambda i, s, *_, j=j: (0, s[j])))
    for row in (own_row, other_row):
        specs.append(pl.BlockSpec((tile, 128), lambda i, s, *_, row=row: (row(i), 0)))
    return specs


def project(acc, tok, pieces, gran):
    own, other, gain, own_scale, other_scale = tok
    rows, width = own.shape
    cols = pieces[0][0].shape[1]
    tile = 384
    tiles = rows // tile
    granules = [len(o) for _, o in pieces]
    n = sum(granules)
    offs = jnp.stack([o for _, os in pieces for o in os]).astype(jnp.int32)
    acc_spec = pl.BlockSpec((tile, cols), lambda i, s: (i, 0))
    in_specs = ([acc_spec] if acc is not None else []) + token_specs(tile, tiles, gran, n)
    for a, _ in pieces:
        in_specs.append(pl.BlockSpec(a.shape, lambda i, s: (0, 0)))
    args = ([acc] if acc is not None else []) + [own] * n + [other] * n + [gain] * n
    args += [own_scale, other_scale] + [a for a, _ in pieces]
    return pl.pallas_call(
        functools.partial(project_kernel, acc is not None, granules, tiles),
        grid_spec=pltpu.PrefetchScalarGridSpec(
            num_scalar_prefetch=1, grid=(2 * tiles,), in_specs=in_specs, out_specs=acc_spec
        ),
        out_shape=jax.ShapeDtypeStruct((2 * rows, cols), jnp.float32),
        compiler_params=pltpu.CompilerParams(vmem_limit_bytes=VMEM_LIMIT),
        cost_estimate=pl.CostEstimate(
            flops=4 * rows * n * gran * cols, bytes_accessed=8 * rows * cols, transcendentals=0
        ),
        name="project",
    )(offs, *args)


def attend_block(keys, values, query, fresh, fresh_values, head, visible, first):
    scale = HD**-0.5
    dims = (((1,), (1,)), ((), ()))
    past = lax.dot_general(query, keys, dims, preferred_element_type=jnp.float32) * scale
    recent = lax.dot_general(query, fresh, dims, preferred_element_type=jnp.float32) * scale
    where = lax.broadcasted_iota(jnp.int32, past.shape, 1)
    past = jnp.where(where < visible, past, masked_score)
    col = lax.broadcasted_iota(jnp.int32, recent.shape, 1) - head * STEPS
    step = lax.broadcasted_iota(jnp.int32, recent.shape, 0) % STEPS
    recent = jnp.where((col >= 0) & (col <= step) & (first > 0), recent, masked_score)
    top = jnp.maximum(
        jnp.max(past, axis=1, keepdims=True), jnp.max(recent, axis=1, keepdims=True)
    )
    past = jnp.exp(past - top)
    recent = jnp.exp(recent - top)
    total = jnp.sum(past, axis=1, keepdims=True) + jnp.sum(recent, axis=1, keepdims=True)
    out = jnp.dot(past.astype(jnp.bfloat16), values, preferred_element_type=jnp.float32)
    out = out + jnp.dot(
        recent.astype(jnp.bfloat16), fresh_values, preferred_element_type=jnp.float32
    )
    return out / total, top + jnp.log(total)


def as_row(column):
    n = column.shape[0]
    eye = lax.broadcasted_iota(jnp.int32, (n, n), 0) == lax.broadcasted_iota(jnp.int32, (n, n), 1)
    return jnp.sum(jnp.where(eye, column, 0.0), axis=0, keepdims=True)


def attend_half(kv, base, table_ref, q_ref, out_ref, blocks):
    stats = []
    for b in range(blocks):
        slot = table_ref[base + b, 0]
        visible = table_ref[base + b, 1]
        first = table_ref[base + b, 2]
        q = q_ref[slot]
        fresh = q[LOCAL_ROWS:]
        turned = jnp.concatenate([fresh[OWN_ROWS // 2 :], fresh[: OWN_ROWS // 2]], axis=0)
        block = kv[b * BLK : (b + 1) * BLK]
        lses = []
        for h in range(LOCAL_KV):
            keys = block[:, h * HD : (h + 1) * HD]
            values = block[:, (LOCAL_KV + h) * HD : (LOCAL_KV + h + 1) * HD]
            query = q[h * ROWS : (h + 1) * ROWS]
            out, lse = attend_block(keys, values, query, fresh, turned, h, visible, first)
            at = b * LOCAL_ROWS + h * ROWS
            out_ref[0, at : at + ROWS, :] = out.astype(jnp.bfloat16)
            lses.append(lse)
        lse = as_row(jnp.concatenate(lses, axis=0))
        high = lse.astype(jnp.bfloat16).astype(jnp.float32)
        mid = (lse - high).astype(jnp.bfloat16).astype(jnp.float32)
        low = lse - high - mid
        stats.append(jnp.concatenate([high, mid], axis=1))
        stats.append(jnp.concatenate([low, jnp.zeros_like(low)], axis=1))
    stats.append(jnp.zeros((STAT_ROWS - 2 * blocks, 2 * LOCAL_ROWS), jnp.float32))
    at = blocks * LOCAL_ROWS
    out_ref[0, at : at + STAT_ROWS, :] = jnp.concatenate(stats, axis=0).astype(jnp.bfloat16)


def attend_kernel(granules, blocks, offs_ref, table_ref, *refs):
    n = sum(granules)
    acc, own, other, gains = refs[0], refs[1 : 1 + n], refs[1 + n : 1 + 2 * n], refs[1 + 2 * n : 1 + 3 * n]
    own_scale, other_scale = refs[1 + 3 * n : 3 + 3 * n]
    pieces, q_ref, out_ref = refs[3 + 3 * n : -2], refs[-2], refs[-1]
    i = pl.program_id(0)

    def run(lhs, scale_ref, base):
        kv = partial_sum(acc[...], lhs, scale_ref, gains, pieces, granules).astype(jnp.bfloat16)
        attend_half(kv, base, table_ref, q_ref, out_ref, blocks)

    @pl.when(i == 0)
    def _():
        run(own, own_scale, 0)

    @pl.when(i == 1)
    def _():
        run(other, other_scale, blocks)


def attend(acc, tok, pieces, gran, table, queries):
    own, other, gain, own_scale, other_scale = tok
    rows, width = own.shape
    cols = acc.shape[1]
    blocks = rows // BLK
    granules = [len(o) for _, o in pieces]
    n = sum(granules)
    offs = jnp.stack([o for _, os in pieces for o in os]).astype(jnp.int32)
    in_specs = [pl.BlockSpec((rows, cols), lambda i, s, t: (i, 0))]
    in_specs += token_specs(rows, 1, gran, n)
    for a, _ in pieces:
        in_specs.append(pl.BlockSpec(a.shape, lambda i, s, t: (0, 0)))
    in_specs.append(pl.BlockSpec(queries.shape, lambda i, s, t: (0, 0, 0)))
    out_rows = blocks * LOCAL_ROWS + STAT_ROWS
    args = [acc] + [own] * n + [other] * n + [gain] * n + [own_scale, other_scale]
    args += [a for a, _ in pieces] + [queries]
    return pl.pallas_call(
        functools.partial(attend_kernel, granules, blocks),
        grid_spec=pltpu.PrefetchScalarGridSpec(
            num_scalar_prefetch=2,
            grid=(2,),
            in_specs=in_specs,
            out_specs=pl.BlockSpec((1, out_rows, HD), lambda i, s, t: (i, 0, 0)),
        ),
        out_shape=jax.ShapeDtypeStruct((2, out_rows, HD), jnp.bfloat16),
        compiler_params=pltpu.CompilerParams(vmem_limit_bytes=VMEM_LIMIT),
        cost_estimate=pl.CostEstimate(
            flops=4 * rows * n * gran * cols, bytes_accessed=8 * rows * cols, transcendentals=0
        ),
        name="attend",
    )(offs, table, *args)


def combine_kernel(halves, blocks, slots, slot_ref, slot_row_ref, *refs):
    ins, out_ref, acc_ref = refs[:-2], refs[-2], refs[-1]
    acc_ref[...] = jnp.zeros_like(acc_ref)
    per = 8
    rows = []
    for a, j in halves:
        stat = ins[a][j, blocks * LOCAL_ROWS :, :].astype(jnp.float32)
        for b in range(blocks):
            high, low = stat[2 * b : 2 * b + 1], stat[2 * b + 1 : 2 * b + 2]
            rows.append(high[:, :LOCAL_ROWS] + high[:, LOCAL_ROWS:] + low[:, :LOCAL_ROWS])
        rows.append(jnp.full((per - blocks, LOCAL_ROWS), masked_score, jnp.float32))
    lse = jnp.concatenate(rows, axis=0)
    lse = jnp.concatenate([lse, jnp.zeros_like(lse)], axis=1)
    lse = jnp.concatenate(
        [lse[k : k + 128].T[:LOCAL_ROWS] for k in range(0, lse.shape[0], 128)], axis=1
    )
    owner = slot_row_ref[...]
    weight = jnp.zeros_like(lse)
    for s in range(slots):
        mine = owner == s
        here = jnp.where(mine, lse, 2 * masked_score)
        top = jnp.max(here, axis=1, keepdims=True)
        grown = jnp.where(mine, jnp.exp(here - top), 0.0)
        total = jnp.sum(grown, axis=1, keepdims=True)
        weight = jnp.where(mine, grown / jnp.maximum(total, 1e-30), weight)
    for e, (a, j) in enumerate(halves):
        for b in range(blocks):
            at = e * per + b
            slot = slot_ref[at]
            part = ins[a][j, b * LOCAL_ROWS : (b + 1) * LOCAL_ROWS, :].astype(jnp.float32)
            acc_ref[slot] = acc_ref[slot] + part * weight[:, at : at + 1]
    for s in range(slots):
        value = acc_ref[s].reshape(LOCAL_ROWS // STEPS, STEPS, HD)
        if s % 4 == 0:
            held = []
        held.append(value)
        if s % 4 == 3:
            out_ref[:, (s - 3) * STEPS : (s + 1) * STEPS, :] = jnp.concatenate(
                held, axis=1
            ).astype(jnp.bfloat16)


def combine(parts, halves, blocks, slots, entry_slots):
    heads = LOCAL_ROWS // STEPS
    entries = entry_slots.shape[0]
    return pl.pallas_call(
        functools.partial(combine_kernel, halves, blocks, slots),
        in_specs=[
            pl.BlockSpec(memory_space=pltpu.SMEM),
            pl.BlockSpec(memory_space=pltpu.VMEM),
        ]
        + [pl.BlockSpec(memory_space=pltpu.VMEM) for _ in parts],
        out_specs=pl.BlockSpec(memory_space=pltpu.VMEM),
        out_shape=jax.ShapeDtypeStruct((heads, slots * STEPS, HD), jnp.bfloat16),
        scratch_shapes=[pltpu.VMEM((slots, LOCAL_ROWS, HD), jnp.float32)],
        compiler_params=pltpu.CompilerParams(vmem_limit_bytes=VMEM_LIMIT),
        name="combine",
    )(entry_slots, entry_slots.reshape(1, entries), *parts)


def out_kernel(has_acc, which_ref, x_ref, w_ref, *refs):
    acc = refs[0][...] if has_acc else None
    for h in range(x_ref.shape[0]):
        term = jnp.dot(
            x_ref[h], w_ref[h * HD : (h + 1) * HD, :], preferred_element_type=jnp.float32
        )
        acc = term if acc is None else acc + term
    refs[-1][...] = acc.astype(refs[-1].dtype)


def out_project(x, w_out, half, acc, dtype):
    heads, rows, _ = x.shape
    cols = w_out.shape[1]
    in_specs = [
        pl.BlockSpec(x.shape, lambda i, s: (0, 0, 0)),
        pl.BlockSpec((heads * HD, cols), lambda i, s: (s[0], 0)),
    ]
    if acc is not None:
        in_specs.append(pl.BlockSpec((rows, cols), lambda i, s: (0, 0)))
    return pl.pallas_call(
        functools.partial(out_kernel, acc is not None),
        grid_spec=pltpu.PrefetchScalarGridSpec(
            num_scalar_prefetch=1,
            grid=(1,),
            in_specs=in_specs,
            out_specs=pl.BlockSpec((rows, cols), lambda i, s: (0, 0)),
        ),
        out_shape=jax.ShapeDtypeStruct((rows, cols), dtype),
        compiler_params=pltpu.CompilerParams(vmem_limit_bytes=VMEM_LIMIT),
        cost_estimate=pl.CostEstimate(
            flops=2 * rows * heads * HD * cols, bytes_accessed=2 * heads * HD * cols,
            transcendentals=0,
        ),
        name="out_project",
    )(half.reshape(1), x, w_out, *([acc] if acc is not None else []))


def block_tables(request_owner, lengths, block_table, n_blocks):
    req_count = request_owner.shape[0]
    req_index = jnp.arange(req_count, dtype=jnp.int32)
    earlier = (request_owner[None, :] == request_owner[:, None]) & (
        req_index[None, :] < req_index[:, None]
    )
    slot_of = request_owner * OWN_MAX + jnp.sum(earlier.astype(jnp.int32), axis=1)
    place = jnp.arange(n_blocks, dtype=jnp.int32) % MAXBLK
    slot = jnp.repeat(slot_of, MAXBLK)
    visible = jnp.clip(jnp.repeat(lengths, MAXBLK) - place * BLK, 0, BLK)
    hit = (block_table[None, :] == jnp.arange(n_blocks, dtype=jnp.int32)[:, None]).astype(jnp.int32)
    values = jnp.stack([slot, visible, (place == 0).astype(jnp.int32)], axis=0)
    return jnp.sum(hit[:, None, :] * values[None, :, :], axis=2)


ORDER = [
    "zB1", "yC", "qp", "c", "qc", "yB0", "zB2", "ex", "zq1", "xB1", "yq0", "pair", "zC1", "yBz1",
    "xC0", "stat", "zB3", "yBx1", "xB2", "inv", "yBz2", "zC2", "xC1", "yq1", "zq2", "xB3", "G1",
    "zC3", "yBz3", "xC2", "yBx2", "zq3", "G2", "xC3", "yq3", "yq2", "yBx3", "G3",
]
WAITS = {
    "ex": ["yC", "qc"], "xC0": ["zB2"], "stat": ["zq1"], "zB3": ["yB0", "xB1", "yq0"],
    "xB2": ["xC0"], "inv": ["yBz1"], "zq2": ["ex", "inv"], "xB3": ["yBx1"], "G1": ["xB2"],
    "zC3": ["yBz2", "xC1", "yq1"], "yBz3": ["zq2"], "zq3": ["xB3"], "xC3": ["yBz3"],
    "yq3": ["yBx2"], "yq2": ["xC2"],
}


def any_order(nz):
    order = ["zB1", "yC", "yB0", "c", "qp", "qc", "yq0", "ex", "stat", "inv", "pair", "xC0"]
    for k in range(1, nz):
        order += [f"xB{k}", f"zC{k}", f"yBz{k}", f"zq{k}"]
        order += [f"zB{k + 1}"] if k < nz - 1 else []
        order += [f"yBx{k}", f"xC{k}", f"yq{k}"]
        order += [f"G{k}"]
    return order


def on_device(
    links, tokens, norm_gain, w_kv, w_out, lengths, request_owner, block_table, dec_query, dec_new
):
    size, nz = links.tensor, links.nz
    me = lax.axis_index("tensor")
    half = lax.axis_index("groups") % 2
    core = me % CORES
    rows = w_kv.shape[0]
    gran = rows // 2
    blocks = tokens.shape[0] // BLK
    n_blocks = block_table.shape[0]
    slots = OWN_MAX * size
    h0, h1 = half, 1 - half

    mine, theirs, mine_half, theirs_half = split_columns(w_kv, core, half)
    got = {}

    def back(k):
        return (me + size - 4 * k) % size

    def queries_here():
        q = dec_query.reshape(OWN_MAX, STEPS, CORES, LOCAL_ROWS // STEPS, HD)
        q = q.transpose(2, 0, 3, 1, 4).reshape(CORES, OWN_MAX, LOCAL_ROWS, HD)
        new = dec_new.reshape(OWN_MAX, STEPS, 2, CORES, LOCAL_KV, HD).transpose(3, 0, 2, 4, 1, 5)
        return jnp.concatenate([q, new.reshape(CORES, OWN_MAX, OWN_ROWS, HD)], axis=2)

    def at(device, halved):
        return device * 2 + halved

    def piece(name):
        if name == "mine":
            return mine, [at(me, 0), at(me, 1)]
        if name == "c":
            return got[name], [at(me ^ 1, 0), at(me ^ 1, 1)]
        if name == "yB0":
            return got[name], [at(me ^ 2, 0), at(me ^ 2, 1)]
        if name == "yC":
            return got[name], [at(me ^ 3, h0)]
        if name == "xC0":
            return got[name], [at(me ^ 3, h1)]
        there = back(int(name[-1]))
        kind = name[:-1]
        where = {
            "zB": [at(there, h0)],
            "xB": [at(there, h1)],
            "yBz": [at(there ^ 2, h0)],
            "yBx": [at(there ^ 2, h1)],
            "zC": [at(there ^ 1, h0), at(there ^ 3, h0)],
            "xC": [at(there ^ 1, h1), at(there ^ 3, h1)],
        }[kind]
        return got[name], where

    def stage(i):
        if i == 1:
            names = ["mine", "c", "yB0", "zB1", "xB1", "yC", "xC0", "zC1"]
        else:
            k = i - 1
            names = [f"yBz{k}", f"yBx{k}", f"zB{k + 1}", f"xB{k + 1}", f"zC{k + 1}", f"xC{k}"]
        return names

    last = [f"yBz{nz - 1}", f"yBx{nz - 1}", f"xC{nz - 1}"]
    acc = None
    order = ORDER if nz == 4 else any_order(nz)
    for name in order:
        waits = [got[w] for w in WAITS.get(name, [])] if nz == 4 else []
        kind, k = name.rstrip("0123456789"), int(name[-1]) if name[-1].isdigit() else 0
        with jax.named_scope(name):
            if kind == "G":
                if k == nz - 1 or nz == 4 and k == 3:
                    names = stage(k)
                else:
                    names = stage(k)
                pieces = [piece(n) for n in names]
                pieces[-1] = (tied(pieces[-1][0], waits), pieces[-1][1])
                acc = project(acc, tok, pieces, gran)
                continue
            if kind == "stat":
                scales = row_scale(tied(tokens, waits))
                continue
            if kind == "qp":
                q = queries_here()
                q_mine = lax.dynamic_index_in_dim(q, core, 0, keepdims=False)
                q_other = lax.dynamic_index_in_dim(q, 1 - core, 0, keepdims=False)
                continue
            if kind == "pair":
                c_half = lax.dynamic_slice_in_dim(got["c"], half * gran, gran, 0)
                got["pair"] = jnp.concatenate([tied(c_half, waits), got["yC"]], 0)
                continue
            if kind == "zq" and k == 1:
                got["zq0"] = jnp.stack([q_mine, got["qc"]])
            sources = {
                "c": theirs,
                "ex": tokens,
                "inv": None if kind != "inv" else scales,
                "qc": None if kind != "qc" else q_other,
                "yC": theirs_half,
                "yB": mine,
                "zB": mine_half if k == 1 else got.get(f"zB{k - 1}"),
                "xB": got.get(f"zB{k}"),
                "yBz": got.get(f"zB{k}"),
                "yBx": got.get(f"xB{k}"),
                "zC": got.get("pair") if k == 1 else got.get(f"zC{k - 1}"),
                "xC": got.get(f"zC{k}") if k else got.get("yC"),
                "zq": got.get(f"zq{k - 1}"),
                "yq": got.get(f"zq{k}"),
            }
            if kind == "yq" and k == 0 and "zq0" not in got:
                got["zq0"] = jnp.stack([q_mine, got["qc"]])
                sources["yq"] = got["zq0"]
            along = {"c": "c", "ex": "c", "inv": "c", "qc": "c", "yC": "yc"}.get(kind, kind[0])
            got[name] = links.move(tied(sources[kind], waits), along)
        if kind == "inv":
            tok = (tokens, got["ex"], norm_gain.reshape(1, -1), scales, got["inv"])

    queries = jnp.stack(
        [jnp.stack([got[f"zq{k}"], got[f"yq{k}"]]) for k in range(nz)]
    ).reshape(slots, QROWS, HD)

    tables = block_tables(request_owner, lengths, block_table, n_blocks)
    chip = jnp.concatenate(
        [
            lax.dynamic_slice_in_dim(tables, me * blocks, blocks, 0),
            lax.dynamic_slice_in_dim(tables, (me ^ 1) * blocks, blocks, 0),
        ]
    )
    slot = chip[:, 0]
    holder = slot // OWN_MAX
    far = holder // CORES
    q_at = (me // 4 - far // 2) % nz * 2 + ((far ^ (me // CORES)) & 1)
    q_at = (q_at * CORES + ((holder ^ me) & 1)) * OWN_MAX + slot % OWN_MAX
    table = jnp.stack([q_at, chip[:, 1], chip[:, 2]], axis=1)
    outs = attend(acc, tok, [piece(n) for n in last], gran, table, queries)

    parts, entries = [], []

    def arrived(value, device):
        entries.extend([(len(parts), 0, device), (len(parts), 1, device ^ 1)])
        parts.append(value)

    arrived(outs, me)
    z_got = {}
    for k in range(1, nz):
        with jax.named_scope(f"oz{k}"):
            z_got[k] = links.move(outs, "z", k)
        arrived(z_got[k], back(k))
    for k in range(nz):
        with jax.named_scope(f"oy{k}"):
            arrived(links.move(z_got[k] if k else outs, "y"), back(k) ^ 2)
    devices = jnp.stack([d for _, _, d in entries])
    entry = jnp.take(tables[:, 0].reshape(size, blocks), devices, axis=0)
    entry = jnp.pad(entry, ((0, 0), (0, 8 - blocks)), constant_values=-1).reshape(-1)
    attended = combine(parts, [(a, j) for a, j, _ in entries], blocks, slots, entry)
    with jax.named_scope("swap_attended"):
        attended_other = links.move(attended, "c")
    total = out_project(attended, w_out, core, None, jnp.float32)
    out = out_project(attended_other, w_out, 1 - core, total, jnp.bfloat16)
    return out.reshape(slots, STEPS, w_out.shape[1])


def solution(mesh):
    placed = (
        P(("groups", "tensor"), None),
        P(),
        P("tensor", None),
        P(None, "tensor"),
        P("groups"),
        P("groups"),
        P("groups"),
        P(("groups", "tensor"), None, None),
        P(("groups", "tensor"), None, None),
    )
    links = Links(mesh.shape["groups"], mesh.shape["tensor"])
    return jax.shard_map(
        functools.partial(on_device, links),
        mesh=mesh,
        in_specs=placed,
        out_specs=P("groups", None, "tensor"),
        check_vma=False,
    )
```

```python
import functools

import jax
import jax.numpy as jnp
from jax import lax
from jax.experimental import pallas as pl
from jax.experimental.pallas import tpu as pltpu
from jax.sharding import PartitionSpec as P

QH = 32
KVH = 4
HD = 128
BLK = 128
MAXBLK = 4
STEPS = 4
OWN_MAX = 2
CORES = 2
LOCAL_KV = KVH // CORES
GROUP = QH // KVH
ROWS = GROUP * STEPS
LOCAL_ROWS = LOCAL_KV * ROWS
OWN_ROWS = 2 * LOCAL_KV * STEPS
QROWS = LOCAL_ROWS + OWN_ROWS
STAT_ROWS = 16

norm_eps = 1e-05
masked_score = -1e30
VMEM_LIMIT = 61 * 1024 * 1024
SMALL = pl.CostEstimate(flops=1024, bytes_accessed=1024, transcendentals=0)


class Links:
    def __init__(self, groups, tensor):
        self.groups, self.tensor = groups, tensor
        self.nz = tensor // 4

    def move(self, value, kind, hops=1):
        pairs = []
        for g in range(self.groups):
            for t in range(self.tensor):
                to_g, to_t = g, t
                if kind == "c":
                    to_t = t ^ 1
                elif kind == "y":
                    to_t = t ^ 2
                elif kind == "yc":
                    to_t = t ^ 3
                elif kind == "z":
                    to_t = (t + 4 * hops) % self.tensor
                else:
                    to_g = g ^ 1
                pairs.append((g * self.tensor + t, to_g * self.tensor + to_t))
        return lax.ppermute(value, ("groups", "tensor"), pairs)


def tied(value, others):
    if not others:
        return value
    return lax.optimization_barrier((value,) + tuple(others))[0]


def split_columns(w_kv, core, half):
    rows, width = w_kv.shape
    part = width // (2 * CORES)
    gran = rows // 2

    def kernel(core_ref, half_ref, a, b, c, d, out_a, out_b, out_c, out_d):
        for src, dst in ((a, out_a), (b, out_b), (c, out_c), (d, out_d)):
            dst[...] = src[...]

    whole, halved = pl.BlockSpec((rows, part), lambda j, c, h: (0, j)), pl.BlockSpec(
        (gran, part), lambda j, c, h: (0, j)
    )
    return pl.pallas_call(
        kernel,
        grid_spec=pltpu.PrefetchScalarGridSpec(
            num_scalar_prefetch=2,
            grid=(2,),
            in_specs=[
                pl.BlockSpec((rows, part), lambda j, c, h: (0, CORES * j + c[0])),
                pl.BlockSpec((rows, part), lambda j, c, h: (0, CORES * j + 1 - c[0])),
                pl.BlockSpec((gran, part), lambda j, c, h: (h[0], CORES * j + c[0])),
                pl.BlockSpec((gran, part), lambda j, c, h: (h[0], CORES * j + 1 - c[0])),
            ],
            out_specs=[whole, whole, halved, halved],
        ),
        out_shape=[
            jax.ShapeDtypeStruct((n, 2 * part), w_kv.dtype) for n in (rows, rows, gran, gran)
        ],
        name="split",
    )(core.reshape(1), half.reshape(1), w_kv, w_kv, w_kv, w_kv)


def row_scale(tokens):
    rows, width = tokens.shape
    tile, chunk = 64, 512
    tiles = rows // tile

    def kernel(tok_hbm, out_ref, tok_ref, sems):
        def load(i):
            at = pl.ds(pl.multiple_of(i * tile, tile), tile)
            return pltpu.make_async_copy(tok_hbm.at[at], tok_ref.at[i], sems.at[i])

        for i in range(tiles):
            load(jnp.int32(i)).start()

        @pl.loop(0, tiles)
        def _(i):
            load(i).wait()
            acc = None
            for c in range(0, width, chunk):
                wide = tok_ref[i, :, c : c + chunk].astype(jnp.float32)
                acc = wide * wide if acc is None else acc + wide * wide
            inverse = lax.rsqrt(jnp.sum(acc, axis=1, keepdims=True) / width + norm_eps)
            at = pl.ds(pl.multiple_of(i * tile, tile), tile)
            out_ref[at, :] = jnp.broadcast_to(inverse, (tile, 128))

    return pl.pallas_call(
        kernel,
        in_specs=[pl.BlockSpec(memory_space=pltpu.HBM)],
        out_specs=pl.BlockSpec(memory_space=pltpu.VMEM),
        out_shape=jax.ShapeDtypeStruct((rows, 128), jnp.float32),
        scratch_shapes=[
            pltpu.VMEM((tiles, tile, width), tokens.dtype),
            pltpu.SemaphoreType.DMA((tiles,)),
        ],
        compiler_params=pltpu.CompilerParams(vmem_limit_bytes=VMEM_LIMIT),
        cost_estimate=SMALL,
        name="row_scale",
    )(tokens)


def partial_sum(acc, lhs, gran, scale, gain_ref, offs_ref, base, w_ref, arrived):
    for j, tokens in enumerate(lhs):
        arrived(j)
        lanes = pl.ds(pl.multiple_of(offs_ref[base + j] * gran, gran), gran)
        wide = tokens[...].astype(jnp.float32)
        normed = (wide * scale * gain_ref[:, lanes]).astype(jnp.bfloat16)
        term = jnp.dot(
            normed, w_ref[j * gran : (j + 1) * gran, :], preferred_element_type=jnp.float32
        )
        acc = term if acc is None else acc + term
    return acc


def piece_copies(pieces, gran, w_ref, sems):
    copies, of_granule, at = [], [], 0
    for i, piece in enumerate(pieces):
        rows = piece.shape[0]
        copies.append(pltpu.make_async_copy(piece, w_ref.at[pl.ds(at, rows)], sems.at[i]))
        of_granule += [i if k == 0 else None for k in range(rows // gran)]
        at += rows
    return copies, of_granule


def project(acc, tok, pieces, gran, offs, base):
    own, other, gain, own_scale, other_scale = tok
    rows, width = own.shape
    cols = pieces[0][0].shape[1]
    tile = 384
    tiles = rows // tile
    total = 2 * tiles
    arrays = [a for a, _ in pieces]
    n = sum(a.shape[0] for a in arrays) // gran
    has_acc = acc is not None

    def kernel(offs_ref, *refs):
        refs = list(refs)
        acc_hbm = refs.pop(0) if has_acc else None
        own_hbm, other_hbm, gain_ref, own_scale_ref, other_scale_ref = refs[:5]
        w_hbm, out_hbm = refs[5 : 5 + len(arrays)], refs[5 + len(arrays)]
        lhs_ref, w_ref, in_ref, out_ref, lhs_sem, w_sem, in_sem, out_sem = refs[6 + len(arrays) :]
        w_copies, of_granule = piece_copies(w_hbm, gran, w_ref, w_sem)

        def loads(source, t, i, slot):
            found = []
            for j in range(n):
                lanes = pl.ds(pl.multiple_of(offs_ref[base + j] * gran, gran), gran)
                found.append(
                    pltpu.make_async_copy(
                        source.at[pl.ds(pl.multiple_of(t * tile, tile), tile), lanes],
                        lhs_ref.at[slot, j],
                        lhs_sem.at[slot, j],
                    )
                )
            return found

        def acc_load(i, slot):
            return pltpu.make_async_copy(
                acc_hbm.at[pl.ds(pl.multiple_of(i * tile, tile), tile)],
                in_ref.at[slot],
                in_sem.at[slot],
            )

        def store(i, slot):
            return pltpu.make_async_copy(
                out_ref.at[slot],
                out_hbm.at[pl.ds(pl.multiple_of(i * tile, tile), tile)],
                out_sem.at[slot],
            )

        def start(i, slot):
            @pl.when(i < tiles)
            def _():
                for copy in loads(own_hbm, i, i, slot):
                    copy.start()

            @pl.when((i >= tiles) & (i < total))
            def _():
                for copy in loads(other_hbm, i - tiles, i, slot):
                    copy.start()

            if has_acc:

                @pl.when(i < total)
                def _():
                    acc_load(i, slot).start()

        start(jnp.int32(0), 0)
        for copy in w_copies:
            copy.start()

        @pl.loop(0, total)
        def _(i):
            slot = lax.rem(i, 2)
            start(i + 1, 1 - slot)

            @pl.when(i == 0)
            def _():
                for copy in w_copies:
                    copy.wait()

            for copy in loads(own_hbm, 0, i, slot):
                copy.wait()
            if has_acc:
                acc_load(i, slot).wait()

            @pl.when(i >= 2)
            def _():
                store(i - 2, slot).wait()

            rows_at = pl.ds(pl.multiple_of(lax.rem(i, tiles) * tile, tile), tile)
            scale = jnp.where(i < tiles, own_scale_ref[rows_at, :], other_scale_ref[rows_at, :])
            result = partial_sum(
                in_ref[slot] if has_acc else None,
                [lhs_ref.at[slot, j] for j in range(n)],
                gran,
                scale[:, :1],
                gain_ref,
                offs_ref,
                base,
                w_ref,
                lambda j: None,
            )
            out_ref[slot] = result
            store(i, slot).start()

        for i in (total - 2, total - 1):
            store(jnp.int32(i), i % 2).wait()

    hbm = pl.BlockSpec(memory_space=pltpu.HBM)
    vmem = pl.BlockSpec(memory_space=pltpu.VMEM)
    args = ([acc] if has_acc else []) + [own, other, gain, own_scale, other_scale] + arrays
    return pl.pallas_call(
        kernel,
        in_specs=[pl.BlockSpec(memory_space=pltpu.SMEM)]
        + ([hbm] if has_acc else [])
        + [hbm, hbm, vmem, vmem, vmem]
        + [hbm for _ in arrays],
        out_specs=hbm,
        out_shape=jax.ShapeDtypeStruct((2 * rows, cols), jnp.float32),
        scratch_shapes=[
            pltpu.VMEM((2, n, tile, gran), jnp.bfloat16),
            pltpu.VMEM((n * gran, cols), jnp.bfloat16),
            pltpu.VMEM((2, tile, cols) if has_acc else (1, 8, 128), jnp.float32),
            pltpu.VMEM((2, tile, cols), jnp.float32),
            pltpu.SemaphoreType.DMA((2, n)),
            pltpu.SemaphoreType.DMA((len(arrays),)),
            pltpu.SemaphoreType.DMA((2,)),
            pltpu.SemaphoreType.DMA((2,)),
        ],
        compiler_params=pltpu.CompilerParams(vmem_limit_bytes=VMEM_LIMIT),
        cost_estimate=SMALL,
        name="project",
    )(offs, *args)


def as_row(column):
    n = column.shape[0]
    eye = lax.broadcasted_iota(jnp.int32, (n, n), 0) == lax.broadcasted_iota(jnp.int32, (n, n), 1)
    return jnp.sum(jnp.where(eye, column, 0.0), axis=0, keepdims=True)


def attend_half(kv, base, table_ref, q_ref, out_ref, blocks):
    scale = HD**-0.5
    dims = (((1,), (1,)), ((), ()))
    seen = BLK + OWN_ROWS
    shape = (LOCAL_ROWS, seen)
    col = lax.broadcasted_iota(jnp.int32, shape, 1)
    row = lax.broadcasted_iota(jnp.int32, shape, 0)
    fresh_col = col - BLK - row // ROWS * STEPS
    causal = (fresh_col >= 0) & (fresh_col <= row % STEPS) & (col >= BLK)
    q_head = lax.broadcasted_iota(jnp.int32, (LOCAL_ROWS, HD), 0) // ROWS
    stats = []
    for b in range(blocks):
        slot = table_ref[base + b, 0]
        visible = table_ref[base + b, 1]
        first = table_ref[base + b, 2]
        q = q_ref[slot]
        fresh = q[LOCAL_ROWS:]
        turned = jnp.concatenate([fresh[OWN_ROWS // 2 :], fresh[: OWN_ROWS // 2]], axis=0)
        block = kv[b * BLK : (b + 1) * BLK]
        keys = jnp.concatenate(
            [block[:, : LOCAL_KV * HD], jnp.concatenate([fresh] * LOCAL_KV, axis=1)], axis=0
        )
        wide = jnp.concatenate(
            [jnp.where(q_head == h, q[:LOCAL_ROWS], 0) for h in range(LOCAL_KV)], axis=1
        )
        score = lax.dot_general(wide, keys, dims, preferred_element_type=jnp.float32) * scale
        score = jnp.where((col < visible) | (causal & (first > 0)), score, masked_score)
        top = jnp.max(score, axis=1, keepdims=True)
        grown = jnp.exp(score - top)
        total = jnp.sum(grown, axis=1, keepdims=True)
        probs = grown.astype(jnp.bfloat16)
        values = jnp.concatenate(
            [block[:, LOCAL_KV * HD :], jnp.concatenate([turned] * LOCAL_KV, axis=1)], axis=0
        )
        out = jnp.dot(probs, values, preferred_element_type=jnp.float32) * (1.0 / total)
        for h in range(LOCAL_KV):
            rows = slice(h * ROWS, (h + 1) * ROWS)
            at = b * LOCAL_ROWS + h * ROWS
            out_ref[at : at + ROWS, :] = out[rows, h * HD : (h + 1) * HD].astype(jnp.bfloat16)
        lse = as_row(top + jnp.log(total))
        high = lse.astype(jnp.bfloat16).astype(jnp.float32)
        mid = (lse - high).astype(jnp.bfloat16).astype(jnp.float32)
        low = lse - high - mid
        stats.append(jnp.concatenate([high, mid], axis=1))
        stats.append(jnp.concatenate([low, jnp.zeros_like(low)], axis=1))
    stats.append(jnp.zeros((STAT_ROWS - 2 * blocks, 2 * LOCAL_ROWS), jnp.float32))
    at = blocks * LOCAL_ROWS
    out_ref[at : at + STAT_ROWS, :] = jnp.concatenate(stats, axis=0).astype(jnp.bfloat16)


def attend(acc, tok, pieces, gran, offs, base, table, queries):
    own, other, gain, own_scale, other_scale = tok
    rows, width = own.shape
    cols = acc.shape[1]
    blocks = rows // BLK
    arrays = [a for a, _ in pieces]
    n = sum(a.shape[0] for a in arrays) // gran
    each = queries[0].shape[0]
    out_rows = blocks * LOCAL_ROWS + STAT_ROWS

    def kernel(offs_ref, table_ref, *refs):
        acc_hbm, own_hbm, other_hbm, gain_ref, own_scale_ref, other_scale_ref = refs[:6]
        refs = refs[6:]
        w_hbm, q_hbm, out_ref = refs[: len(arrays)], refs[len(arrays) : -8], refs[-8]
        lhs_ref, w_ref, acc_ref, q_ref, lhs_sem, w_sem, q_sem = refs[-7:]
        w_copies, of_granule = piece_copies(w_hbm, gran, w_ref, w_sem)
        q_copies = [
            pltpu.make_async_copy(q, q_ref.at[pl.ds(i * each, each)], q_sem.at[i])
            for i, q in enumerate(q_hbm)
        ]
        loads = []
        for side, source in enumerate((own_hbm, other_hbm)):
            found = [
                pltpu.make_async_copy(
                    acc_hbm.at[pl.ds(side * rows, rows)], acc_ref.at[side], lhs_sem.at[side, n]
                )
            ]
            for j in range(n):
                lanes = pl.ds(pl.multiple_of(offs_ref[base + j] * gran, gran), gran)
                found.append(
                    pltpu.make_async_copy(
                        source.at[:, lanes], lhs_ref.at[side, j], lhs_sem.at[side, j]
                    )
                )
            loads.append(found)
        for copy in loads[0] + w_copies + q_copies + loads[1]:
            copy.start()
        for side, scale_ref in enumerate((own_scale_ref, other_scale_ref)):
            loads[side][0].wait()

            def arrived(j):
                loads[side][1 + j].wait()
                if side == 0 and of_granule[j] is not None:
                    w_copies[of_granule[j]].wait()

            kv = partial_sum(
                acc_ref[side],
                [lhs_ref.at[side, j] for j in range(n)],
                gran,
                scale_ref[:, :1],
                gain_ref,
                offs_ref,
                base,
                w_ref,
                arrived,
            ).astype(jnp.bfloat16)
            if side == 0:
                for copy in q_copies:
                    copy.wait()
            attend_half(kv, side * blocks, table_ref, q_ref, out_ref.at[side], blocks)

    hbm = pl.BlockSpec(memory_space=pltpu.HBM)
    vmem = pl.BlockSpec(memory_space=pltpu.VMEM)
    smem = pl.BlockSpec(memory_space=pltpu.SMEM)
    return pl.pallas_call(
        kernel,
        in_specs=[smem, smem, hbm, hbm, hbm, vmem, vmem, vmem] + [hbm] * (len(arrays) + len(queries)),
        out_specs=vmem,
        out_shape=jax.ShapeDtypeStruct((2, out_rows, HD), jnp.bfloat16),
        scratch_shapes=[
            pltpu.VMEM((2, n, rows, gran), jnp.bfloat16),
            pltpu.VMEM((n * gran, cols), jnp.bfloat16),
            pltpu.VMEM((2, rows, cols), jnp.float32),
            pltpu.VMEM((each * len(queries), QROWS, HD), jnp.bfloat16),
            pltpu.SemaphoreType.DMA((2, n + 1)),
            pltpu.SemaphoreType.DMA((len(arrays),)),
            pltpu.SemaphoreType.DMA((len(queries),)),
        ],
        compiler_params=pltpu.CompilerParams(vmem_limit_bytes=VMEM_LIMIT),
        cost_estimate=SMALL,
        name="attend",
    )(offs, table, acc, own, other, gain, own_scale, other_scale, *arrays, *queries)


def weight_copies(w_hbm, w_ref, sems, side, heads, group):
    copies = []
    for i, h in enumerate(range(0, heads, group)):
        at = pl.multiple_of(side * heads * HD + h * HD, HD)
        copies.append(
            pltpu.make_async_copy(
                w_hbm.at[pl.ds(at, group * HD)], w_ref.at[pl.ds(h * HD, group * HD)], sems.at[i]
            )
        )
    return copies


def times_weights(x_ref, w_ref, copies, group, total):
    for i, copy in enumerate(copies):
        copy.wait()
        h = i * group
        x = jnp.concatenate([x_ref[h + k] for k in range(group)], axis=1)
        term = jnp.dot(
            x, w_ref[h * HD : (h + group) * HD, :], preferred_element_type=jnp.float32
        )
        total = term if total is None else total + term
    return total


def combine(parts, halves, blocks, slots, entry_slots, w_out, core):
    heads = LOCAL_ROWS // STEPS
    entries = entry_slots.shape[0]
    cols = w_out.shape[1]
    group = 4
    per = 8

    def kernel(core_ref, slot_ref, slot_row_ref, w_hbm, *refs):
        ins = refs[: len(parts)]
        out_ref, product_ref, acc_ref, w_ref, sems = refs[len(parts) :]
        copies = weight_copies(w_hbm, w_ref, sems, core_ref[0], heads, group)
        for copy in copies:
            copy.start()
        acc_ref[...] = jnp.zeros_like(acc_ref)
        rows = []
        for a, j in halves:
            stat = ins[a][j, blocks * LOCAL_ROWS :, :].astype(jnp.float32)
            for b in range(blocks):
                high, low = stat[2 * b : 2 * b + 1], stat[2 * b + 1 : 2 * b + 2]
                rows.append(high[:, :LOCAL_ROWS] + high[:, LOCAL_ROWS:] + low[:, :LOCAL_ROWS])
            rows.append(jnp.full((per - blocks, LOCAL_ROWS), masked_score, jnp.float32))
        lse = jnp.concatenate(rows, axis=0)
        lse = jnp.concatenate([lse, jnp.zeros_like(lse)], axis=1)
        lse = jnp.concatenate(
            [lse[k : k + 128].T[:LOCAL_ROWS] for k in range(0, lse.shape[0], 128)], axis=1
        )
        owner = slot_row_ref[...]
        weight = jnp.zeros_like(lse)
        for s in range(slots):
            mine = owner == s
            here = jnp.where(mine, lse, 2 * masked_score)
            top = jnp.max(here, axis=1, keepdims=True)
            grown = jnp.where(mine, jnp.exp(here - top), 0.0)
            total = jnp.sum(grown, axis=1, keepdims=True)
            weight = jnp.where(mine, grown / jnp.maximum(total, 1e-30), weight)
        for e, (a, j) in enumerate(halves):
            for b in range(blocks):
                at = e * per + b
                slot = slot_ref[at]
                part = ins[a][j, b * LOCAL_ROWS : (b + 1) * LOCAL_ROWS, :].astype(jnp.float32)
                acc_ref[slot] = acc_ref[slot] + part * weight[:, at : at + 1]
        held = []
        for s in range(slots):
            held.append(acc_ref[s].reshape(heads, STEPS, HD))
            if s % 4 == 3:
                out_ref[:, (s - 3) * STEPS : (s + 1) * STEPS, :] = jnp.concatenate(
                    held, axis=1
                ).astype(jnp.bfloat16)
                held = []
        product_ref[...] = times_weights(out_ref, w_ref, copies, group, None)

    vmem = pl.BlockSpec(memory_space=pltpu.VMEM)
    smem = pl.BlockSpec(memory_space=pltpu.SMEM)
    hbm = pl.BlockSpec(memory_space=pltpu.HBM)
    return pl.pallas_call(
        kernel,
        in_specs=[smem, smem, vmem, hbm] + [vmem for _ in parts],
        out_specs=[vmem, vmem],
        out_shape=[
            jax.ShapeDtypeStruct((heads, slots * STEPS, HD), jnp.bfloat16),
            jax.ShapeDtypeStruct((slots * STEPS, cols), jnp.float32),
        ],
        scratch_shapes=[
            pltpu.VMEM((slots, LOCAL_ROWS, HD), jnp.float32),
            pltpu.VMEM((heads * HD, cols), jnp.bfloat16),
            pltpu.SemaphoreType.DMA((heads // group,)),
        ],
        compiler_params=pltpu.CompilerParams(vmem_limit_bytes=24 * 1024 * 1024),
        name="combine",
    )(core.reshape(1), entry_slots, entry_slots.reshape(1, entries), w_out, *parts)


def out_project(product, other, w_out, core, slots):
    heads, rows, _ = other.shape
    cols = w_out.shape[1]
    group = 4

    def kernel(core_ref, product_ref, other_ref, w_hbm, out_ref, w_ref, sems):
        copies = weight_copies(w_hbm, w_ref, sems, 1 - core_ref[0], heads, group)
        for copy in copies:
            copy.start()
        total = times_weights(other_ref, w_ref, copies, group, product_ref[...])
        out_ref[...] = total.reshape(slots, STEPS, cols).astype(jnp.bfloat16)

    vmem = pl.BlockSpec(memory_space=pltpu.VMEM)
    return pl.pallas_call(
        kernel,
        in_specs=[
            pl.BlockSpec(memory_space=pltpu.SMEM),
            vmem,
            vmem,
            pl.BlockSpec(memory_space=pltpu.HBM),
        ],
        out_specs=vmem,
        out_shape=jax.ShapeDtypeStruct((slots, STEPS, cols), jnp.bfloat16),
        scratch_shapes=[
            pltpu.VMEM((heads * HD, cols), jnp.bfloat16),
            pltpu.SemaphoreType.DMA((heads // group,)),
        ],
        compiler_params=pltpu.CompilerParams(vmem_limit_bytes=24 * 1024 * 1024),
        name="out_project",
    )(core.reshape(1), product, other, w_out)


def block_tables(request_owner, lengths, block_table, n_blocks):
    req_count = request_owner.shape[0]
    req_index = jnp.arange(req_count, dtype=jnp.int32)
    earlier = (request_owner[None, :] == request_owner[:, None]) & (
        req_index[None, :] < req_index[:, None]
    )
    slot_of = request_owner * OWN_MAX + jnp.sum(earlier.astype(jnp.int32), axis=1)
    place = jnp.arange(n_blocks, dtype=jnp.int32) % MAXBLK
    slot = jnp.repeat(slot_of, MAXBLK)
    visible = jnp.clip(jnp.repeat(lengths, MAXBLK) - place * BLK, 0, BLK)
    hit = (block_table[None, :] == jnp.arange(n_blocks, dtype=jnp.int32)[:, None]).astype(jnp.int32)
    values = jnp.stack([slot, visible, (place == 0).astype(jnp.int32)], axis=0)
    return jnp.sum(hit[:, None, :] * values[None, :, :], axis=2)


ORDER = [
    "zB3", "yC", "c", "yB0", "zB1", "ex", "qp", "pair", "zC1", "xC0", "xB1", "stat", "zB2",
    "yBz3", "xC1", "inv", "qc", "zC3", "yq", "yBz1", "xB2", "zC2", "yBx1", "xB3", "qq", "xC3",
    "yBz2", "G1", "zq1", "yBx3", "xC2", "yBx2", "zq3", "zq2", "G2",
]
WAITS = {
    "xC0": ["zB3"],
    "zB2": ["yB0", "stat"],
    "yBz3": ["xC0"],
    "inv": ["xB1"],
    "zC3": ["inv"],
    "yBz1": ["zB2"],
    "xB2": ["yBz3"],
    "zC2": ["yq"],
    "yBx1": ["xC1"],
    "xB3": ["yBz1"],
    "yBz2": ["xB2"],
    "zq1": ["yBx1", "G1"],
    "yBx2": ["yBz2"],
    "zq3": ["xC3"],
    "ex": ["c"],
    "qc": ["ex"],
}
CHAIN = True
STAGES = [
    ["mine", "c", "yB0", "zB1", "zB2", "zB3", "yC", "xB1", "xC0", "zC1"],
    ["xB2", "xB3", "yBz1", "yBz3", "yBz2", "yBx1", "zC3", "xC1", "zC2"],
    ["yBx2", "yBx3", "xC3", "xC2"],
]


def ring(nz):
    both = zip(range(1, nz // 2 + 1), range(nz - 1, nz // 2 - 1, -1))
    return list(dict.fromkeys(k for pair in both for k in pair))


def any_order(nz):
    ks = ring(nz)
    order = ["zB1", "yC", "c", "yB0", "ex", "qp", "qc", "stat", "inv", "pair", "xC0", "yq", "qq"]
    order += [f"zB{k}" for k in ks if k != 1]
    for k in ks:
        order += [f"xB{k}", f"zC{k}", f"yBz{k}"]
    order += ["G1"]
    for k in ks:
        order += [f"zq{k}", f"yBx{k}", f"xC{k}"]
    return order + ["G2"]


def any_stages(nz):
    ks = range(1, nz)
    return [
        ["mine", "c", "yB0", "yC", "xC0"] + [f"zB{k}" for k in ks],
        [f"{n}{k}" for k in ks for n in ("xB", "yBz", "zC")],
        [f"{n}{k}" for k in ks for n in ("yBx", "xC")],
    ]


def on_device(
    links, tokens, norm_gain, w_kv, w_out, lengths, request_owner, block_table, dec_query, dec_new
):
    size, nz = links.tensor, links.nz
    me = lax.axis_index("tensor")
    half = lax.axis_index("groups") % 2
    core = me % CORES
    rows = w_kv.shape[0]
    gran = rows // 2
    blocks = tokens.shape[0] // BLK
    n_blocks = block_table.shape[0]
    slots = OWN_MAX * size
    h0, h1 = half, 1 - half

    mine, theirs, mine_half, theirs_half = split_columns(w_kv, core, half)
    got = {}

    def back(k):
        return (me + size - 4 * k) % size

    def queries_here():
        q = dec_query.reshape(OWN_MAX, STEPS, CORES, LOCAL_ROWS // STEPS, HD)
        q = q.transpose(2, 0, 3, 1, 4).reshape(CORES, OWN_MAX, LOCAL_ROWS, HD)
        new = dec_new.reshape(OWN_MAX, STEPS, 2, CORES, LOCAL_KV, HD).transpose(3, 0, 2, 4, 1, 5)
        return jnp.concatenate([q, new.reshape(CORES, OWN_MAX, OWN_ROWS, HD)], axis=2)

    def at(device, halved):
        return device * 2 + halved

    def places(name):
        if name == "mine":
            return [at(me, 0), at(me, 1)]
        if name == "c":
            return [at(me ^ 1, 0), at(me ^ 1, 1)]
        if name == "yB0":
            return [at(me ^ 2, 0), at(me ^ 2, 1)]
        if name == "yC":
            return [at(me ^ 3, h0)]
        if name == "xC0":
            return [at(me ^ 3, h1)]
        there = back(int(name[-1]))
        kind = name[:-1]
        return {
            "zB": [at(there, h0)],
            "xB": [at(there, h1)],
            "yBz": [at(there ^ 2, h0)],
            "yBx": [at(there ^ 2, h1)],
            "zC": [at(there ^ 1, h0), at(there ^ 3, h0)],
            "xC": [at(there ^ 1, h1), at(there ^ 3, h1)],
        }[kind]

    def piece(name):
        return got[name], places(name)

    stages = STAGES if nz == 4 else any_stages(nz)
    where = [[p for n in names for p in places(n)] for names in stages]
    bases = [sum(len(w) for w in where[:i]) for i in range(len(where))]
    offs = jnp.stack([p for w in where for p in w]).astype(jnp.int32)
    got["mine"] = mine
    tables = block_tables(request_owner, lengths, block_table, n_blocks)
    chip = jnp.concatenate(
        [
            lax.dynamic_slice_in_dim(tables, me * blocks, blocks, 0),
            lax.dynamic_slice_in_dim(tables, (me ^ 1) * blocks, blocks, 0),
        ]
    )
    slot = chip[:, 0]
    holder = slot // OWN_MAX
    far = holder // CORES
    q_at = (me // 4 - far // 2) % nz * 2 + ((far ^ (me // CORES)) & 1)
    q_at = (q_at * CORES + ((holder ^ me) & 1)) * OWN_MAX + slot % OWN_MAX
    table = jnp.stack([q_at, chip[:, 1], chip[:, 2]], axis=1)
    devices = [back(k) ^ other for other in (0, 2) for k in range(nz)]
    devices = jnp.stack([d ^ j for d in devices for j in range(2)])
    entry = jnp.take(tables[:, 0].reshape(size, blocks), devices, axis=0)
    entry = jnp.pad(entry, ((0, 0), (0, 8 - blocks)), constant_values=-1).reshape(-1)
    offs, table, entry, ready = lax.optimization_barrier((offs, table, entry, tokens))
    acc = None
    order = ORDER if nz == 4 else any_order(nz)
    chain = []
    for name in order:
        waits = (chain if CHAIN else []) + ([got[w] for w in WAITS.get(name, [])] if nz == 4 else [])
        kind, k = name.rstrip("0123456789"), int(name[-1]) if name[-1].isdigit() else 0
        with jax.named_scope(name):
            if kind == "G":
                pieces = [piece(n) for n in stages[k - 1]]
                pieces[-1] = (tied(pieces[-1][0], waits), pieces[-1][1])
                chain = [pieces[-1][0]]
                acc = got[name] = project(acc, tok, pieces, gran, offs, bases[k - 1])
                continue
            if kind == "stat":
                chain = [tied(ready, waits)]
                scales = got["stat"] = row_scale(chain[0])
                continue
            if kind == "qp":
                q = tied(queries_here(), waits)
                chain = [q]
                q_mine = lax.dynamic_index_in_dim(q, core, 0, keepdims=False)
                q_other = lax.dynamic_index_in_dim(q, 1 - core, 0, keepdims=False)
                continue
            if kind == "pair":
                c_half = lax.dynamic_slice_in_dim(got["c"], half * gran, gran, 0)
                chain = [tied(c_half, waits)]
                got["pair"] = jnp.concatenate([chain[0], got["yC"]], 0)
                continue
            if kind == "qq":
                got["qq"] = jnp.concatenate([chip_q, tied(got["yq"], waits)])
                continue
            if kind == "yq":
                chip_q = jnp.concatenate([q_mine, got["qc"]])
            hop = 1 if k <= nz // 2 else -1
            before = k - hop
            first = before % nz == 0
            sources = {
                "c": theirs,
                "ex": tokens,
                "inv": None if kind != "inv" else scales,
                "qc": None if kind != "qc" else q_other,
                "yC": theirs_half,
                "yB": mine,
                "zB": mine_half if first else got.get(f"zB{before}"),
                "xB": got.get(f"zB{k}"),
                "yBz": got.get(f"zB{k}"),
                "yBx": got.get(f"xB{k}"),
                "zC": got.get("pair") if first else got.get(f"zC{before}"),
                "xC": got.get(f"zC{k}") if k else got.get("yC"),
                "zq": got.get("qq") if first else got.get(f"zq{before}"),
                "yq": None if kind != "yq" else chip_q,
            }
            along = {"c": "c", "ex": "c", "inv": "c", "qc": "c", "yC": "yc"}.get(kind, kind[0])
            chain = [tied(sources[kind], waits)]
            got[name] = links.move(chain[0], along, hop)
        if kind == "inv":
            tok = (tokens, got["ex"], norm_gain.reshape(1, -1), scales, got["inv"])

    queries = [got["qq"]] + [got[f"zq{k}"] for k in range(1, nz)]

    outs = attend(
        acc, tok, [piece(n) for n in stages[-1]], gran, offs, bases[-1], table, queries
    )

    z_got, y_got = {0: outs}, {}
    for k in ring(nz):
        hop = 1 if k <= nz // 2 else -1
        with jax.named_scope(f"oz{k}"):
            z_got[k] = links.move(z_got[(k - hop) % nz], "z", hop)
    for k in [0] + ring(nz):
        with jax.named_scope(f"oy{k}"):
            early = [y_got[0]] if k == 1 else []
            y_got[k] = links.move(tied(z_got[k], early), "y")
    parts = [got_from[k] for got_from in (z_got, y_got) for k in range(nz)]
    halves = [(i, j) for i in range(len(parts)) for j in range(2)]
    attended, product = combine(parts, halves, blocks, slots, entry, w_out, core)
    with jax.named_scope("swap_attended"):
        attended_other = links.move(attended, "c")
    return out_project(product, attended_other, w_out, core, slots)


def solution(mesh):
    placed = (
        P(("groups", "tensor"), None),
        P(),
        P("tensor", None),
        P(None, "tensor"),
        P("groups"),
        P("groups"),
        P("groups"),
        P(("groups", "tensor"), None, None),
        P(("groups", "tensor"), None, None),
    )
    links = Links(mesh.shape["groups"], mesh.shape["tensor"])
    return jax.shard_map(
        functools.partial(on_device, links),
        mesh=mesh,
        in_specs=placed,
        out_specs=P("groups", None, "tensor"),
        check_vma=False,
    )
```
